512 devices in a mesh: fsdp: 64 (over y, x, core), tensor: 8 (over z).
Axes of the slice: x: 4, y: 8, z: 8, core: 2. Of those that a mesh axis runs over, the one named last changes fastest.
Arguments:
- grad: bfloat16 [16384, 8192], P('tensor', 'fsdp'), may hold values from -0.26953125 to 0.26953125
- owner: int32 [4, 8], replicated, may hold values from 0 to 7, each once within a row
- codes: int32 [2, 16384, 8192], P(None, 'tensor', 'fsdp'), may hold values from 0 to 15
- scale_ids: int32 [2, 128, 8192], P(None, 'tensor', 'fsdp'), may hold values from 0 to 15
- scale_table: float32 [16], replicated, may hold values from 0.1 to 1
Outputs:
- statistics: float32 [2, 16384, 8192], P(None, 'tensor', 'fsdp')
The draws below stay inside these ranges and needn't reach their ends.
Inputs may be any that keep to these rules, and one draw needn't show every extreme that they name: Each row owner[c] holds every slot 0 to 7 once: block row r of block column c keeps its statistics at slot owner[c, r].
All inputs are finite; a program needn't handle non-finite values.
Results may differ from the reference program's by a relative error of at most 0.0003.
Values may be sent and summed in bfloat16 or wider, within the bound.
No kernel may reach another device: no remote copies, remote signals or barrier semaphores. Data moves between devices by JAX's collectives and lax.ppermute only.
A program may use at most 64 MiB of HBM per device.

```python
import math
import jax
import jax.numpy as jnp
from jax import lax

D = 8192
B = 2048
FF_WIN = 16384
QG = 128
LEVELS = 16
NBR = 8
NCB = 4


def touch_ends(values, key, smallest, largest):
    place = [jax.random.randint(jax.random.fold_in(key, axis), (), 0, length) for axis, length in enumerate(values.shape)]
    longest = values.shape.index(max(values.shape))
    next_to = place[:longest] + [(place[longest] + 1) % values.shape[longest]] + place[longest + 1:]
    return values.at[tuple(place)].set(smallest).at[tuple(next_to)].set(largest)


def steps_of(own_key, extent, cuts, low, largest):
    def one(position, parts):
        heights = jax.random.uniform(jax.random.fold_in(jax.random.fold_in(own_key, 6), position), (parts,), jnp.float32, low / len(cuts), largest / len(cuts))
        return jnp.repeat(jnp.exp(heights), extent[position] // parts).reshape((-1,) + (1,) * (len(extent) - position - 1))

    factor_of = one(*cuts[0])
    for cut in cuts[1:]:
        factor_of = factor_of * one(*cut)
    return factor_of


def centred(stream_key, dims, spread, most, shards=(), held_as=jnp.bfloat16):
    gain = steps_of(stream_key, dims, shards, -0.22, 0.18) if shards else 1.0
    array = jax.random.normal(stream_key, dims, jnp.float32) * spread * gain
    return jnp.minimum(jnp.maximum(array, -most), most).astype(held_as)


def setup_inputs(seed: int = 0) -> dict:
    key_list = jax.random.split(jax.random.key(seed), 6)
    grad = centred(key_list[0], (FF_WIN, D), 0.045, 0.26953125, ((0, 8), (1, 64)))
    owner = jax.vmap(lambda own: jax.random.permutation(own, NBR))(jax.random.split(key_list[1], NCB)).reshape((NCB, NBR)).astype(jnp.int32)
    codes = touch_ends(jax.random.randint(key_list[2], (2, FF_WIN, D), 0, 16), jax.random.fold_in(key_list[2], 1), 0, 15).astype(jnp.int32)
    scale_ids = touch_ends(jax.random.randint(key_list[3], (2, FF_WIN // QG, D), 0, LEVELS), jax.random.fold_in(key_list[3], 1), 0, LEVELS - 1).astype(jnp.int32)
    scale_table = jnp.clip(jnp.exp(jax.random.uniform(key_list[4], (LEVELS,), jnp.float32, math.log(0.1), math.log(1.0))), 0.1, 1.0)
    return {"grad": grad, "owner": owner, "codes": codes, "scale_ids": scale_ids, "scale_table": scale_table}


def gram_pair(single_block):
    left_gram = jnp.dot(single_block, single_block.T, precision=lax.Precision.HIGHEST)
    right_gram = jnp.dot(single_block.T, single_block, precision=lax.Precision.HIGHEST)
    return jnp.stack([left_gram, right_gram])


def reference(grad, owner, codes, scale_ids, scale_table):
    slot_rows = jnp.argsort(owner, axis=1).astype(jnp.int32)
    blocks = grad.astype(jnp.float32).reshape(NBR, B, NCB, B).transpose(2, 0, 1, 3)
    placed = jax.vmap(lambda column_blocks, order_row: column_blocks[order_row])(blocks, slot_rows)
    flat_blocks = placed.reshape(NCB * NBR, B, B)
    result = lax.map(gram_pair, flat_blocks).reshape(NCB, NBR, 2, B, B)
    stacked = result.transpose(2, 1, 3, 0, 4).reshape(2, NBR * B, NCB * B)
    scale_grid = jnp.repeat(scale_table[scale_ids], QG, axis=1)
    previous = scale_grid * ((codes.astype(jnp.float32) - 7.5) / 7.5)
    return 0.9 * previous + 0.1 * stacked
```

```python
import functools

import jax
import jax.numpy as jnp
from jax import lax
from jax.experimental import pallas as pl
from jax.experimental.pallas import tpu as pltpu
from jax.sharding import Mesh
from jax.sharding import PartitionSpec as P

B = 2048
PLANE = ("y", "x", "core")


def place_kernel(owner_ref, block_ref, in_ref, out_ref):
    column_block = block_ref[0]
    for row_block in range(in_ref.shape[0]):
        slot = owner_ref[column_block, row_block]
        out_ref[pl.ds(slot, 1)] = in_ref[row_block : row_block + 1]


def place(chunks, owner, column_block):
    return pl.pallas_call(
        place_kernel,
        out_shape=jax.ShapeDtypeStruct(chunks.shape, chunks.dtype),
        in_specs=[
            pl.BlockSpec(memory_space=pltpu.SMEM),
            pl.BlockSpec(memory_space=pltpu.SMEM),
            pl.BlockSpec(memory_space=pltpu.VMEM),
        ],
        out_specs=pl.BlockSpec(memory_space=pltpu.VMEM),
    )(owner, column_block, chunks)


def shards(grad, owner, codes, scale_ids, scale_table):
    rows_here, width_here = grad.shape
    slots = lax.axis_size("tensor")
    column_block = lax.axis_index("c")
    member = lax.axis_index(PLANE)
    chunks = grad.reshape(slots, rows_here // slots, width_here)
    spread = lax.all_to_all(chunks, "tensor", 0, 0, tiled=True)
    placed = place(spread, owner, column_block.reshape(1))
    own = lax.all_to_all(placed, "tensor", 0, 0, tiled=True).reshape(rows_here, width_here)
    pieces = lax.all_gather(own, PLANE, axis=0)
    own_rows = lax.dynamic_slice_in_dim(pieces, member * width_here, width_here, 1)
    left = jnp.einsum("nkc,nic->ki", pieces, own_rows, preferred_element_type=jnp.float32)
    right = jnp.einsum("nkc,kd->ncd", pieces, own, preferred_element_type=jnp.float32)
    stacked = jnp.stack([left, right.reshape(rows_here, width_here)])
    group_rows = rows_here // scale_ids.shape[1]
    level_index = jnp.arange(scale_table.shape[0], dtype=jnp.int32)
    scale_grid = jnp.sum(jnp.where(scale_ids[..., None] == level_index, scale_table, 0.0), axis=-1)
    previous = scale_grid[:, :, None, :] * (
        (codes.reshape(2, -1, group_rows, width_here).astype(jnp.float32) - 7.5) / 7.5
    )
    return 0.9 * previous.reshape(2, rows_here, width_here) + 0.1 * stacked


def solution(mesh):
    fine = Mesh(
        mesh.devices.reshape(4, 2, 4, 2, 8), ("c", "y", "x", "core", "tensor")
    )
    fsdp = ("c", "y", "x", "core")
    in_specs = (P("tensor", fsdp), P(), P(None, "tensor", fsdp), P(None, "tensor", fsdp), P())
    out_specs = P(None, "tensor", fsdp)
    return jax.shard_map(shards, mesh=fine, in_specs=in_specs, out_specs=out_specs, check_vma=False)
```

```python
import functools

import jax
import jax.numpy as jnp
from jax import lax
from jax.experimental import pallas as pl
from jax.experimental.pallas import tpu as pltpu
from jax.sharding import Mesh
from jax.sharding import PartitionSpec as P

B = 2048
W = 128
CHIPS = 8
VMEM = pl.BlockSpec(memory_space=pltpu.VMEM)
SMEM = pl.BlockSpec(memory_space=pltpu.SMEM)
PARAMS = pltpu.CompilerParams(vmem_limit_bytes=40 * 2**20)
f32 = jnp.float32
bf16 = jnp.bfloat16


def place_kernel(owner_ref, block_ref, in_ref, out_ref):
    column_block = block_ref[0]
    for row_block in range(in_ref.shape[0]):
        slot = owner_ref[column_block, row_block]
        out_ref[pl.ds(slot, 1)] = in_ref[row_block : row_block + 1]


def place(chunks, owner, column_block):
    return pl.pallas_call(
        place_kernel,
        out_shape=jax.ShapeDtypeStruct(chunks.shape, chunks.dtype),
        in_specs=[SMEM, SMEM, VMEM],
        out_specs=VMEM,
        compiler_params=PARAMS,
    )(owner, column_block, chunks)


def dequant_kernel(table_ref, codes_ref, ids_ref, out_ref):
    ids = ids_ref[...]
    scale = jnp.zeros(ids.shape, f32)
    for level in range(table_ref.shape[0]):
        scale = jnp.where(ids == level, table_ref[level], scale)
    group_rows = codes_ref.shape[1] // ids.shape[1]
    for side in range(2):
        for group in range(ids.shape[1]):
            rows = slice(group * group_rows, (group + 1) * group_rows)
            code = codes_ref[side, rows, :].astype(f32)
            out_ref[side, rows, :] = 0.9 * (scale[side, group : group + 1] * ((code - 7.5) / 7.5))


def dequant(scale_table, codes, scale_ids):
    return pl.pallas_call(
        dequant_kernel,
        out_shape=jax.ShapeDtypeStruct(codes.shape, f32),
        in_specs=[SMEM, VMEM, VMEM],
        out_specs=VMEM,
        compiler_params=PARAMS,
        cost_estimate=pl.CostEstimate(flops=2**22, bytes_accessed=2**22, transcendentals=0),
    )(scale_table, codes, scale_ids)


def gram_kernel(at_ref, own_ref, other_ref, *refs):
    pieces, (keep_ref, send_ref, block, pair, rows) = refs[:CHIPS], refs[CHIPS:]
    own_row = pl.multiple_of(at_ref[0], W)
    other_row = pl.multiple_of(at_ref[1], W)
    for i, piece in enumerate(pieces):
        block[:, i * W : (i + 1) * W] = piece[...]
    pair[:, :W] = own_ref[...]
    pair[:, W:] = other_ref[...]
    rows[:W, :] = block[pl.ds(own_row, W), :]
    rows[W:, :] = block[pl.ds(other_row, W), :]
    for start in range(0, B, 512):
        left = lax.dot_general(
            block[start : start + 512, :],
            rows[...],
            (((1,), (1,)), ((), ())),
            preferred_element_type=f32,
        )
        keep_ref[start : start + 512, :] = left[:, :W]
        send_ref[start : start + 512, :] = left[:, W:]
    for i in range(0, CHIPS, 2):
        right = lax.dot_general(
            block[:, i * W : (i + 2) * W],
            pair[...],
            (((0,), (0,)), ((), ())),
            preferred_element_type=f32,
        )
        for j in range(2):
            start = pl.multiple_of(at_ref[2 + i + j], W)
            keep_ref[pl.ds(start, W), :] = right[j * W : (j + 1) * W, :W]
            send_ref[pl.ds(start, W), :] = right[j * W : (j + 1) * W, W:]


def grams(at, own, other, pieces):
    out = jax.ShapeDtypeStruct((B + CHIPS * W, W), f32)
    return pl.pallas_call(
        gram_kernel,
        out_shape=(out, out),
        in_specs=[SMEM] + [VMEM] * (2 + CHIPS),
        out_specs=(VMEM, VMEM),
        scratch_shapes=[
            pltpu.VMEM((B, CHIPS * W), bf16),
            pltpu.VMEM((B, 2 * W), bf16),
            pltpu.VMEM((2 * W, CHIPS * W), bf16),
        ],
        compiler_params=PARAMS,
        cost_estimate=pl.CostEstimate(flops=2**31, bytes_accessed=2**23, transcendentals=0),
    )(at, own, other, *pieces)


def blend_kernel(core_ref, base_ref, keep_ref, got_ref, out_ref):
    out_ref[0] = base_ref[0] + 0.1 * (keep_ref[:B, :] + got_ref[:B, :])
    core = core_ref[0]
    for chip in range(CHIPS):
        rows = slice(B + chip * W, B + (chip + 1) * W)
        for part_ref, parity in ((keep_ref, core), (got_ref, 1 - core)):
            to = pl.ds(pl.multiple_of((2 * chip + parity) * W, W), W)
            out_ref[1, to, :] = base_ref[1, to, :] + 0.1 * part_ref[rows, :]


def blend(core, base, keep, got):
    return pl.pallas_call(
        blend_kernel,
        out_shape=jax.ShapeDtypeStruct(base.shape, f32),
        in_specs=[SMEM, VMEM, VMEM, VMEM],
        out_specs=VMEM,
        compiler_params=PARAMS,
    )(core, base, keep, got)


def ring(value, direction):
    pairs = [
        (x * 2 + core, (x + direction * (1 - 2 * core)) % 4 * 2 + core)
        for x in range(4)
        for core in range(2)
    ]
    return lax.ppermute(value, ("x", "core"), pairs)


def swap(value, axis):
    return lax.ppermute(value, axis, [(0, 1), (1, 0)])


def shards(grad, owner, codes, scale_ids, scale_table):
    rows_here, width_here = grad.shape
    slots = lax.axis_size("tensor")
    y, x, core = (lax.axis_index(name) for name in ("y", "x", "core"))
    chunks = grad.reshape(slots, rows_here // slots, width_here)
    spread = lax.all_to_all(chunks, "tensor", 0, 0, tiled=True)
    placed = place(spread, owner, lax.axis_index("c").reshape(1))
    own = lax.all_to_all(placed, "tensor", 0, 0, tiled=True).reshape(rows_here, width_here)
    base = dequant(scale_table, codes, scale_ids)

    behind = ring(own, 1)
    across = swap(own, "y")
    ahead = ring(own, -1)
    other = swap(own, "core")
    behind, ahead, across = lax.optimization_barrier((behind, ahead, across))
    across_ahead = ring(across, -1)
    far = ring(behind, 1)
    across_behind = swap(behind, "y")
    across_far = ring(across_ahead, -1)
    pieces = [own, behind, ahead, far, across, across_behind, across_ahead, across_far]

    step = 1 - 2 * core
    xs = [x, x - step, x + step, x + 2]
    chip = [y * 4 + at % 4 for at in xs] + [(1 - y) * 4 + at % 4 for at in xs]
    at = jnp.stack(
        [(chip[0] * 2 + core) * W, (chip[0] * 2 + 1 - core) * W] + [B + at * W for at in chip]
    ).astype(jnp.int32)
    keep, send = grams(at, own, other, pieces)
    return blend(core.reshape(1), base, keep, swap(send, "core"))


def solution(mesh):
    fine = Mesh(mesh.devices.reshape(4, 2, 4, 2, 8), ("c", "y", "x", "core", "tensor"))
    fsdp = ("c", "y", "x", "core")
    in_specs = (P("tensor", fsdp), P(), P(None, "tensor", fsdp), P(None, "tensor", fsdp), P())
    out_specs = P(None, "tensor", fsdp)
    return jax.shard_map(shards, mesh=fine, in_specs=in_specs, out_specs=out_specs, check_vma=False)
```

```python
import functools

import jax
import jax.numpy as jnp
from jax import lax
from jax.experimental import pallas as pl
from jax.experimental.pallas import tpu as pltpu
from jax.sharding import Mesh
from jax.sharding import PartitionSpec as P

B = 2048
W = 128
FIRST, SECOND = 4, 3
DEQ = 2**36
STRIP = 512
VMEM = pl.BlockSpec(memory_space=pltpu.VMEM)
SMEM = pl.BlockSpec(memory_space=pltpu.SMEM)
PARAMS = pltpu.CompilerParams(vmem_limit_bytes=40 * 2**20)
f32 = jnp.float32
bf16 = jnp.bfloat16


def place_kernel(owner_ref, block_ref, in_ref, out_ref):
    column_block = block_ref[0]
    for row_block in range(in_ref.shape[0]):
        slot = owner_ref[column_block, row_block]
        out_ref[pl.ds(slot, 1)] = in_ref[row_block : row_block + 1]


def place(chunks, owner, column_block):
    return pl.pallas_call(
        place_kernel,
        out_shape=jax.ShapeDtypeStruct(chunks.shape, chunks.dtype),
        in_specs=[SMEM, SMEM, VMEM],
        out_specs=VMEM,
        compiler_params=PARAMS,
    )(owner, column_block, chunks)


def dequant_kernel(table_ref, codes_ref, ids_ref, out_ref):
    ids = ids_ref[...]
    scale = jnp.zeros(ids.shape, f32)
    for level in range(table_ref.shape[0]):
        scale = jnp.where(ids == level, table_ref[level], scale)
    group_rows = codes_ref.shape[1] // ids.shape[1]
    for side in range(2):
        for group in range(ids.shape[1]):
            rows = slice(group * group_rows, (group + 1) * group_rows)
            code = codes_ref[side, rows, :].astype(f32)
            out_ref[side, rows, :] = 0.9 * (scale[side, group : group + 1] * ((code - 7.5) / 7.5))


def dequant(scale_table, codes, scale_ids):
    return pl.pallas_call(
        dequant_kernel,
        out_shape=jax.ShapeDtypeStruct(codes.shape, f32),
        in_specs=[SMEM, VMEM, VMEM],
        out_specs=VMEM,
        compiler_params=PARAMS,
        cost_estimate=pl.CostEstimate(flops=DEQ, bytes_accessed=2**22, transcendentals=0),
    )(scale_table, codes, scale_ids)


def left_of(block, rows, start):
    return lax.dot_general(
        block[start : start + STRIP, :],
        rows[...],
        (((1,), (1,)), ((), ())),
        preferred_element_type=f32,
    )


def right_of(piece, pair):
    return lax.dot_general(piece, pair, (((0,), (0,)), ((), ())), preferred_element_type=f32)


def collect(at_ref, pieces, block, rows):
    for i, piece in enumerate(pieces):
        block[:, i * W : (i + 1) * W] = piece[...]
    for i in range(2):
        rows[i * W : (i + 1) * W, :] = block[pl.ds(pl.multiple_of(at_ref[i], W), W), :]


def first_kernel(at_ref, *refs):
    pieces, (left_ref, block, rows) = refs[:FIRST], refs[FIRST:]
    collect(at_ref, pieces, block, rows)
    for start in range(0, B, STRIP):
        left_ref[start : start + STRIP, :] = left_of(block, rows, start)


def first_grams(at, pieces):
    return pl.pallas_call(
        first_kernel,
        out_shape=jax.ShapeDtypeStruct((B, 2 * W), f32),
        in_specs=[SMEM] + [VMEM] * FIRST,
        out_specs=VMEM,
        scratch_shapes=[pltpu.VMEM((B, FIRST * W), bf16), pltpu.VMEM((2 * W, FIRST * W), bf16)],
        compiler_params=PARAMS,
        cost_estimate=pl.CostEstimate(flops=2**30, bytes_accessed=2**22, transcendentals=0),
    )(at, *pieces)


def second_kernel(at_ref, other_ref, left_ref, *refs):
    pieces = refs[: FIRST + SECOND]
    keep_ref, send_ref, block, pair, rows = refs[FIRST + SECOND :]
    collect(at_ref, pieces[FIRST:], block, rows)
    pair[:, :W] = pieces[0][...]
    pair[:, W:] = other_ref[...]
    for start in range(0, B, STRIP):
        to = slice(start, start + STRIP)
        left = left_ref[to, :] + left_of(block, rows, start)
        keep_ref[to, :] = left[:, :W]
        send_ref[to, :] = left[:, W:]
    for i, piece in enumerate(pieces):
        to = slice(B + i * W, B + (i + 1) * W)
        right = right_of(piece[...], pair[...])
        keep_ref[to, :] = right[:, :W]
        send_ref[to, :] = right[:, W:]


def second_grams(at, other, left, pieces):
    out = jax.ShapeDtypeStruct((B + (FIRST + SECOND) * W, W), f32)
    return pl.pallas_call(
        second_kernel,
        out_shape=(out, out),
        in_specs=[SMEM] + [VMEM] * (2 + FIRST + SECOND),
        out_specs=(VMEM, VMEM),
        scratch_shapes=[
            pltpu.VMEM((B, SECOND * W), bf16),
            pltpu.VMEM((B, 2 * W), bf16),
            pltpu.VMEM((2 * W, SECOND * W), bf16),
        ],
        compiler_params=PARAMS,
        cost_estimate=pl.CostEstimate(flops=2**30, bytes_accessed=2**22, transcendentals=0),
    )(at, other, left, *pieces)


def finish_kernel(at_ref, base_ref, keep_ref, got_ref, own_ref, last_ref, got_last_ref, out_ref, block, rows):
    block[:, :W] = last_ref[...]
    block[:, W:] = got_last_ref[...]
    rows[...] = block[pl.ds(pl.multiple_of(at_ref[0], W), W), :]
    for start in range(0, B, STRIP):
        to = slice(start, start + STRIP)
        left = keep_ref[to, :] + got_ref[to, :] + left_of(block, rows, start)
        out_ref[0, to, :] = base_ref[0, to, :] + 0.1 * left
    right = right_of(block[...], own_ref[...])
    early = FIRST + SECOND
    for side, part_ref in enumerate((keep_ref, got_ref)):
        for i in range(early + 1):
            to = pl.ds(pl.multiple_of(at_ref[2 + side * (early + 1) + i], W), W)
            if i < early:
                part = part_ref[B + i * W : B + (i + 1) * W, :]
            else:
                part = right[side * W : (side + 1) * W, :]
            out_ref[1, to, :] = base_ref[1, to, :] + 0.1 * part


def finish(at, base, keep, got, own, last, got_last):
    return pl.pallas_call(
        finish_kernel,
        out_shape=jax.ShapeDtypeStruct(base.shape, f32),
        in_specs=[SMEM] + [VMEM] * 6,
        out_specs=VMEM,
        scratch_shapes=[pltpu.VMEM((B, 2 * W), bf16), pltpu.VMEM((W, 2 * W), bf16)],
        compiler_params=PARAMS,
    )(at, base, keep, got, own, last, got_last)


def ring(value, direction):
    pairs = [
        (x * 2 + core, (x + direction * (1 - 2 * core)) % 4 * 2 + core)
        for x in range(4)
        for core in range(2)
    ]
    return lax.ppermute(value, ("x", "core"), pairs)


def swap(value, axis):
    return lax.ppermute(value, axis, [(0, 1), (1, 0)])


def shards(grad, owner, codes, scale_ids, scale_table):
    rows_here, width_here = grad.shape
    slots = lax.axis_size("tensor")
    y, x, core = (lax.axis_index(name) for name in ("y", "x", "core"))
    chunks = grad.reshape(slots, rows_here // slots, width_here)
    spread = lax.all_to_all(chunks, "tensor", 0, 0, tiled=True)
    placed = place(spread, owner, lax.axis_index("c").reshape(1))
    own = lax.all_to_all(placed, "tensor", 0, 0, tiled=True).reshape(rows_here, width_here)
    base = dequant(scale_table, codes, scale_ids)

    def row_starts(core):
        step = 1 - 2 * core
        xs = [x, x - step, x + step, x, x + 2, x - step, x + step, x + 2]
        ys = [y, y, y, 1 - y, y, 1 - y, 1 - y, 1 - y]
        return [((row * 4 + column % 4) * 2 + core) * W for row, column in zip(ys, xs)]

    mine, theirs = row_starts(core), row_starts(1 - core)
    at = jnp.stack([mine[0], theirs[0]] + mine + theirs).astype(jnp.int32)
    across = swap(own, "y")
    behind = ring(own, 1)
    ahead = ring(own, -1)
    across_behind = swap(behind, "y")
    other = swap(lax.optimization_barrier((own, behind))[0], "core")
    ahead, other = lax.optimization_barrier((ahead, other))
    across_ahead = ring(across, -1)
    far = ring(ahead, -1)
    left = first_grams(at, [own, behind, ahead, across])
    left, across_ahead = lax.optimization_barrier((left, across_ahead))
    across_far = ring(across_ahead, -1)
    pieces = [own, behind, ahead, across, far, across_behind, across_ahead]
    keep, send = second_grams(at, other, left, pieces)
    got, got_far = swap(send, "core"), swap(across_far, "core")
    return finish(at, base, keep, got, own, across_far, got_far)


def solution(mesh):
    fine = Mesh(mesh.devices.reshape(4, 2, 4, 2, 8), ("c", "y", "x", "core", "tensor"))
    fsdp = ("c", "y", "x", "core")
    in_specs = (P("tensor", fsdp), P(), P(None, "tensor", fsdp), P(None, "tensor", fsdp), P())
    out_specs = P(None, "tensor", fsdp)
    return jax.shard_map(shards, mesh=fine, in_specs=in_specs, out_specs=out_specs, check_vma=False)
```

```python
import functools

import jax
import jax.numpy as jnp
from jax import lax
from jax.experimental import pallas as pl
from jax.experimental.pallas import tpu as pltpu
from jax.sharding import Mesh
from jax.sharding import PartitionSpec as P

B = 2048
W = 128
FIRST, MIDDLE, SECOND = 4, 5, 3
STRIP = 512
WEIGHT = 2**36
VMEM = pl.BlockSpec(memory_space=pltpu.VMEM)
SMEM = pl.BlockSpec(memory_space=pltpu.SMEM)
PARAMS = pltpu.CompilerParams(vmem_limit_bytes=20 * 2**20)
f32 = jnp.float32
bf16 = jnp.bfloat16


def place_kernel(slots_ref, in_ref, out_ref):
    for row_block in range(in_ref.shape[0]):
        out_ref[pl.ds(slots_ref[row_block], 1)] = in_ref[row_block : row_block + 1]


def place(chunks, slots):
    return pl.pallas_call(
        place_kernel,
        out_shape=jax.ShapeDtypeStruct(chunks.shape, chunks.dtype),
        in_specs=[SMEM, VMEM],
        out_specs=VMEM,
        compiler_params=PARAMS,
    )(slots, chunks)


def dequant_kernel(table_ref, codes_ref, ids_ref, out_ref):
    ids = ids_ref[0]
    scale = jnp.zeros(ids.shape, f32)
    for level in range(table_ref.shape[0]):
        scale = jnp.where(ids == level, table_ref[level], scale)
    group_rows = codes_ref.shape[1] // ids.shape[0]
    for group in range(ids.shape[0]):
        rows = slice(group * group_rows, (group + 1) * group_rows)
        code = codes_ref[0, rows, :].astype(f32)
        out_ref[rows, :] = 0.9 * (scale[group : group + 1] * ((code - 7.5) / 7.5))


def dequant(side, scale_table, codes, scale_ids):
    def block(array):
        return pl.BlockSpec((1, *array.shape[1:]), lambda i: (side, 0, 0))

    return pl.pallas_call(
        dequant_kernel,
        grid=(1,),
        out_shape=jax.ShapeDtypeStruct(codes.shape[1:], f32),
        in_specs=[SMEM, block(codes), block(scale_ids)],
        out_specs=pl.BlockSpec(codes.shape[1:], lambda i: (0, 0)),
        compiler_params=PARAMS,
        cost_estimate=pl.CostEstimate(flops=WEIGHT, bytes_accessed=2**21, transcendentals=0),
    )(scale_table, codes, scale_ids)


def left_of(block, rows, start):
    return lax.dot_general(
        block[start : start + STRIP, :],
        rows[...],
        (((1,), (1,)), ((), ())),
        preferred_element_type=f32,
    )


def right_of(piece, pair):
    return lax.dot_general(piece, pair, (((0,), (0,)), ((), ())), preferred_element_type=f32)


def collect(at_ref, pieces, block, rows):
    for i, piece in enumerate(pieces):
        block[:, i * W : (i + 1) * W] = piece[...]
    for i in range(2):
        rows[i * W : (i + 1) * W, :] = block[pl.ds(pl.multiple_of(at_ref[i], W), W), :]


def first_kernel(at_ref, *refs):
    pieces, (left_ref, block, rows) = refs[:FIRST], refs[FIRST:]
    collect(at_ref, pieces, block, rows)
    for start in range(0, B, STRIP):
        left_ref[start : start + STRIP, :] = left_of(block, rows, start)


def first_grams(at, pieces):
    return pl.pallas_call(
        first_kernel,
        out_shape=jax.ShapeDtypeStruct((B, 2 * W), f32),
        in_specs=[SMEM] + [VMEM] * FIRST,
        out_specs=VMEM,
        scratch_shapes=[pltpu.VMEM((B, FIRST * W), bf16), pltpu.VMEM((2 * W, FIRST * W), bf16)],
        compiler_params=PARAMS,
        cost_estimate=pl.CostEstimate(flops=2**30, bytes_accessed=2**22, transcendentals=0),
    )(at, *pieces)


def middle_kernel(own_ref, other_ref, *refs):
    pieces, (right_ref, pair) = refs[:MIDDLE], refs[MIDDLE:]
    pair[:, :W] = own_ref[...]
    pair[:, W:] = other_ref[...]
    for i, piece in enumerate(pieces):
        right_ref[i * W : (i + 1) * W, :] = right_of(piece[...], pair[...])


def middle_grams(own, other, pieces):
    return pl.pallas_call(
        middle_kernel,
        out_shape=jax.ShapeDtypeStruct((MIDDLE * W, 2 * W), f32),
        in_specs=[VMEM] * (2 + MIDDLE),
        out_specs=VMEM,
        scratch_shapes=[pltpu.VMEM((B, 2 * W), bf16)],
        compiler_params=PARAMS,
        cost_estimate=pl.CostEstimate(flops=2**30, bytes_accessed=2**22, transcendentals=0),
    )(own, other, *pieces)


def second_kernel(at_ref, own_ref, other_ref, left_ref, right_ref, *refs):
    pieces, (keep_ref, send_ref, block, pair, rows) = refs[:SECOND], refs[SECOND:]
    collect(at_ref, pieces, block, rows)
    pair[:, :W] = own_ref[...]
    pair[:, W:] = other_ref[...]
    for start in range(0, B, STRIP):
        to = slice(start, start + STRIP)
        left = left_ref[to, :] + left_of(block, rows, start)
        keep_ref[to, :] = left[:, :W]
        send_ref[to, :] = left[:, W:]
    middle = B + MIDDLE * W
    keep_ref[B:middle, :] = right_ref[:, :W]
    send_ref[B:middle, :] = right_ref[:, W:]
    for i, piece in enumerate(pieces[MIDDLE - FIRST :]):
        to = slice(middle + i * W, middle + (i + 1) * W)
        right = right_of(piece[...], pair[...])
        keep_ref[to, :] = right[:, :W]
        send_ref[to, :] = right[:, W:]


def second_grams(at, own, other, left, right, pieces):
    out = jax.ShapeDtypeStruct((B + (FIRST + SECOND) * W, W), f32)
    return pl.pallas_call(
        second_kernel,
        out_shape=(out, out),
        in_specs=[SMEM] + [VMEM] * (4 + SECOND),
        out_specs=(VMEM, VMEM),
        scratch_shapes=[
            pltpu.VMEM((B, SECOND * W), bf16),
            pltpu.VMEM((B, 2 * W), bf16),
            pltpu.VMEM((2 * W, SECOND * W), bf16),
        ],
        compiler_params=PARAMS,
        cost_estimate=pl.CostEstimate(flops=2**30, bytes_accessed=2**22, transcendentals=0),
    )(at, own, other, left, right, *pieces)


def sum_kernel(at_ref, base_left, base_right, keep_ref, got_ref, own_ref, last_ref, left_ref, right_ref, rows):
    rows[...] = last_ref[pl.ds(pl.multiple_of(at_ref[0], W), W), :]
    for start in range(0, B, STRIP):
        to = slice(start, start + STRIP)
        left = keep_ref[to, :] + got_ref[to, :] + left_of(last_ref, rows, start)
        left_ref[to, :] = base_left[to, :] + 0.1 * left
    last = right_of(last_ref[...], own_ref[...])
    early = FIRST + SECOND
    for side, part_ref in enumerate((keep_ref, got_ref)):
        for i in range(early + 1 - side):
            to = pl.ds(pl.multiple_of(at_ref[2 + side * (early + 1) + i], W), W)
            part = part_ref[B + i * W : B + (i + 1) * W, :] if i < early else last
            right_ref[to, :] = base_right[to, :] + 0.1 * part
    to = pl.ds(pl.multiple_of(at_ref[2 + 2 * early + 1], W), W)
    right_ref[to, :] = base_right[to, :]


def sum_up(at, base_left, base_right, keep, got, own, last):
    out = jax.ShapeDtypeStruct(base_left.shape, f32)
    return pl.pallas_call(
        sum_kernel,
        out_shape=(out, out),
        in_specs=[SMEM] + [VMEM] * 6,
        out_specs=(VMEM, VMEM),
        scratch_shapes=[pltpu.VMEM((W, W), bf16)],
        compiler_params=PARAMS,
        cost_estimate=pl.CostEstimate(flops=WEIGHT, bytes_accessed=2**22, transcendentals=0),
    )(at, base_left, base_right, keep, got, own, last)


def finish_kernel(at_ref, left_ref, right_ref, own_ref, last_ref, out_ref, result, rows, sems):
    result[1] = right_ref[...]
    to = pl.ds(pl.multiple_of(at_ref[2 + 2 * (FIRST + SECOND) + 1], W), W)
    result[1, to, :] = right_ref[to, :] + 0.1 * right_of(last_ref[...], own_ref[...])
    copies = [pltpu.make_async_copy(result.at[1], out_ref.at[1], sems.at[0])]
    copies[0].start()
    rows[...] = last_ref[pl.ds(pl.multiple_of(at_ref[0], W), W), :]
    for i, start in enumerate(range(0, B, STRIP)):
        to = slice(start, start + STRIP)
        result[0, to, :] = left_ref[to, :] + 0.1 * left_of(last_ref, rows, start)
        copies.append(
            pltpu.make_async_copy(
                result.at[0, pl.ds(start, STRIP)], out_ref.at[0, pl.ds(start, STRIP)], sems.at[1 + i]
            )
        )
        copies[-1].start()
    for copy in copies:
        copy.wait()


def finish(at, left, right, own, last):
    return pl.pallas_call(
        finish_kernel,
        out_shape=jax.ShapeDtypeStruct((2, *left.shape), f32),
        in_specs=[SMEM] + [VMEM] * 4,
        out_specs=pl.BlockSpec(memory_space=pl.ANY),
        scratch_shapes=[
            pltpu.VMEM((2, *left.shape), f32),
            pltpu.VMEM((W, W), bf16),
            pltpu.SemaphoreType.DMA((1 + B // STRIP,)),
        ],
        compiler_params=PARAMS,
    )(at, left, right, own, last)


def ring(value, direction):
    pairs = [
        (x * 2 + core, (x + direction * (1 - 2 * core)) % 4 * 2 + core)
        for x in range(4)
        for core in range(2)
    ]
    return lax.ppermute(value, ("x", "core"), pairs)


def swap(value, axis):
    return lax.ppermute(value, axis, [(0, 1), (1, 0)])


def shards(grad, owner, codes, scale_ids, scale_table):
    rows_here, width_here = grad.shape
    slots = lax.axis_size("tensor")
    y, x, core = (lax.axis_index(name) for name in ("y", "x", "core"))
    chunks = grad.reshape(slots, rows_here // slots, width_here)
    spread = lax.all_to_all(chunks, "tensor", 0, 0, tiled=True)
    owner_row = lax.dynamic_index_in_dim(owner, lax.axis_index("c"), 0, keepdims=False)
    placed = place(spread, owner_row)
    own = lax.all_to_all(placed, "tensor", 0, 0, tiled=True).reshape(rows_here, width_here)
    base_left, base_right = (dequant(side, scale_table, codes, scale_ids) for side in range(2))

    def row_starts(core):
        step = 1 - 2 * core
        xs = [x, x - step, x + step, x, x - step, x + step, x + 2, x + 2]
        ys = [y, y, y, 1 - y, 1 - y, 1 - y, y, 1 - y]
        return [((row * 4 + column % 4) * 2 + core) * W for row, column in zip(ys, xs)]

    mine, theirs = row_starts(core), row_starts(1 - core)
    at = jnp.stack([mine[0], theirs[0]] + mine + theirs).astype(jnp.int32)
    across = swap(own, "y")
    behind = ring(own, 1)
    ahead = ring(own, -1)
    other = swap(own, "core")
    across, base_left = lax.optimization_barrier((across, base_left))
    across_ahead = ring(across, -1)
    behind, base_left = lax.optimization_barrier((behind, base_left))
    across_behind = swap(behind, "y")
    ahead, other, behind = lax.optimization_barrier((ahead, other, behind))
    far = ring(ahead, -1)
    left = first_grams(at, [own, behind, ahead, across])
    left, across_ahead = lax.optimization_barrier((left, across_ahead))
    across_far = ring(across_ahead, -1)
    right = middle_grams(own, other, [own, behind, ahead, across, across_behind])
    keep, send = second_grams(at, own, other, left, right, [across_behind, across_ahead, far])
    got, got_far = swap(send, "core"), swap(across_far, "core")
    left, right = sum_up(at, base_left, base_right, keep, got, own, across_far)
    return finish(at, left, right, own, got_far)


def solution(mesh):
    fine = Mesh(mesh.devices.reshape(4, 2, 4, 2, 8), ("c", "y", "x", "core", "tensor"))
    fsdp = ("c", "y", "x", "core")
    in_specs = (P("tensor", fsdp), P(), P(None, "tensor", fsdp), P(None, "tensor", fsdp), P())
    out_specs = P(None, "tensor", fsdp)
    return jax.shard_map(shards, mesh=fine, in_specs=in_specs, out_specs=out_specs, check_vma=False)
```

```python
import functools

import jax
import jax.numpy as jnp
from jax import lax
from jax.experimental import pallas as pl
from jax.experimental.pallas import tpu as pltpu
from jax.sharding import Mesh
from jax.sharding import PartitionSpec as P

B = 2048
W = 128
FIRST, MIDDLE, SECOND = 4, 5, 3
STRIP = 512
ORDERS = ((0, 4, 2, 6, 1, 5, 3, 7), (0, 4, 6, 2, 7, 3, 5, 1))
WEIGHT = 2**36
VMEM = pl.BlockSpec(memory_space=pltpu.VMEM)
SMEM = pl.BlockSpec(memory_space=pltpu.SMEM)
PARAMS = pltpu.CompilerParams(vmem_limit_bytes=20 * 2**20)
f32 = jnp.float32
bf16 = jnp.bfloat16


def place_kernel(places_ref, in_ref, out_ref):
    for i in range(in_ref.shape[0]):
        out_ref[pl.ds(places_ref[i], 1)] = in_ref[i : i + 1]


def place(chunks, places):
    return pl.pallas_call(
        place_kernel,
        out_shape=jax.ShapeDtypeStruct(chunks.shape, chunks.dtype),
        in_specs=[SMEM, VMEM],
        out_specs=VMEM,
        compiler_params=PARAMS,
    )(places, chunks)


def exchange(chunks):
    groups = [[core * len(order) + z for z in order] for core, order in enumerate(ORDERS)]
    return lax.all_to_all(chunks, ("core", "tensor"), 0, 0, axis_index_groups=groups, tiled=True)


def destinations(owner_row, core):
    order = jnp.where(core == 0, jnp.asarray(ORDERS[0], jnp.int32), jnp.asarray(ORDERS[1], jnp.int32))
    places = jnp.arange(order.shape[0], dtype=jnp.int32)
    slots = jnp.sum(jnp.where(order[:, None] == places, owner_row, 0), axis=1)
    return jnp.sum(jnp.where(slots[:, None] == order, places, 0), axis=1)


def dequant_kernel(table_ref, codes_ref, ids_ref, out_ref):
    ids = ids_ref[0]
    scale = jnp.zeros(ids.shape, f32)
    for level in range(table_ref.shape[0]):
        scale = jnp.where(ids == level, table_ref[level], scale)
    group_rows = codes_ref.shape[1] // ids.shape[0]
    for group in range(ids.shape[0]):
        rows = slice(group * group_rows, (group + 1) * group_rows)
        code = codes_ref[0, rows, :].astype(f32)
        out_ref[rows, :] = 0.9 * (scale[group : group + 1] * ((code - 7.5) / 7.5))


def dequant(side, scale_table, codes, scale_ids):
    def block(array):
        return pl.BlockSpec((1, *array.shape[1:]), lambda i: (side, 0, 0))

    return pl.pallas_call(
        dequant_kernel,
        grid=(1,),
        out_shape=jax.ShapeDtypeStruct(codes.shape[1:], f32),
        in_specs=[SMEM, block(codes), block(scale_ids)],
        out_specs=pl.BlockSpec(codes.shape[1:], lambda i: (0, 0)),
        compiler_params=PARAMS,
        cost_estimate=pl.CostEstimate(flops=WEIGHT, bytes_accessed=2**21, transcendentals=0),
    )(scale_table, codes, scale_ids)


def left_of(block, rows, start):
    return lax.dot_general(
        block[start : start + STRIP, :],
        rows[...],
        (((1,), (1,)), ((), ())),
        preferred_element_type=f32,
    )


def right_of(piece, pair):
    return lax.dot_general(piece, pair, (((0,), (0,)), ((), ())), preferred_element_type=f32)


def collect(at_ref, pieces, block, rows):
    for i, piece in enumerate(pieces):
        block[:, i * W : (i + 1) * W] = piece[...]
    for i in range(2):
        rows[i * W : (i + 1) * W, :] = block[pl.ds(pl.multiple_of(at_ref[i], W), W), :]


def first_kernel(at_ref, *refs):
    pieces, (left_ref, block, rows) = refs[:FIRST], refs[FIRST:]
    collect(at_ref, pieces, block, rows)
    for start in range(0, B, STRIP):
        left_ref[start : start + STRIP, :] = left_of(block, rows, start)


def first_grams(at, pieces):
    return pl.pallas_call(
        first_kernel,
        out_shape=jax.ShapeDtypeStruct((B, 2 * W), f32),
        in_specs=[SMEM] + [VMEM] * FIRST,
        out_specs=VMEM,
        scratch_shapes=[pltpu.VMEM((B, FIRST * W), bf16), pltpu.VMEM((2 * W, FIRST * W), bf16)],
        compiler_params=PARAMS,
        cost_estimate=pl.CostEstimate(flops=2**30, bytes_accessed=2**22, transcendentals=0),
    )(at, *pieces)


def middle_kernel(own_ref, other_ref, *refs):
    pieces, (right_ref, pair) = refs[:MIDDLE], refs[MIDDLE:]
    pair[:, :W] = own_ref[...]
    pair[:, W:] = other_ref[...]
    for i, piece in enumerate(pieces):
        right_ref[i * W : (i + 1) * W, :] = right_of(piece[...], pair[...])


def middle_grams(own, other, pieces):
    return pl.pallas_call(
        middle_kernel,
        out_shape=jax.ShapeDtypeStruct((MIDDLE * W, 2 * W), f32),
        in_specs=[VMEM] * (2 + MIDDLE),
        out_specs=VMEM,
        scratch_shapes=[pltpu.VMEM((B, 2 * W), bf16)],
        compiler_params=PARAMS,
        cost_estimate=pl.CostEstimate(flops=2**30, bytes_accessed=2**22, transcendentals=0),
    )(own, other, *pieces)


def second_kernel(at_ref, own_ref, other_ref, left_ref, right_ref, *refs):
    pieces, (keep_ref, send_ref, block, pair, rows) = refs[:SECOND], refs[SECOND:]
    collect(at_ref, pieces, block, rows)
    pair[:, :W] = own_ref[...]
    pair[:, W:] = other_ref[...]
    for start in range(0, B, STRIP):
        to = slice(start, start + STRIP)
        left = left_ref[to, :] + left_of(block, rows, start)
        keep_ref[to, :] = left[:, :W]
        send_ref[to, :] = left[:, W:]
    middle = B + MIDDLE * W
    keep_ref[B:middle, :] = right_ref[:, :W]
    send_ref[B:middle, :] = right_ref[:, W:]
    for i, piece in enumerate(pieces[MIDDLE - FIRST :]):
        to = slice(middle + i * W, middle + (i + 1) * W)
        right = right_of(piece[...], pair[...])
        keep_ref[to, :] = right[:, :W]
        send_ref[to, :] = right[:, W:]


def second_grams(at, own, other, left, right, pieces):
    out = jax.ShapeDtypeStruct((B + (FIRST + SECOND) * W, W), f32)
    return pl.pallas_call(
        second_kernel,
        out_shape=(out, out),
        in_specs=[SMEM] + [VMEM] * (4 + SECOND),
        out_specs=(VMEM, VMEM),
        scratch_shapes=[
            pltpu.VMEM((B, SECOND * W), bf16),
            pltpu.VMEM((B, 2 * W), bf16),
            pltpu.VMEM((2 * W, SECOND * W), bf16),
        ],
        compiler_params=PARAMS,
        cost_estimate=pl.CostEstimate(flops=2**30, bytes_accessed=2**22, transcendentals=0),
    )(at, own, other, left, right, *pieces)


def sum_kernel(at_ref, base_left, base_right, keep_ref, got_ref, own_ref, last_ref, left_ref, right_ref, rows):
    rows[...] = last_ref[pl.ds(pl.multiple_of(at_ref[0], W), W), :]
    for start in range(0, B, STRIP):
        to = slice(start, start + STRIP)
        left = keep_ref[to, :] + got_ref[to, :] + left_of(last_ref, rows, start)
        left_ref[to, :] = base_left[to, :] + 0.1 * left
    last = right_of(last_ref[...], own_ref[...])
    early = FIRST + SECOND
    for side, part_ref in enumerate((keep_ref, got_ref)):
        for i in range(early + 1 - side):
            to = pl.ds(pl.multiple_of(at_ref[2 + side * (early + 1) + i], W), W)
            part = part_ref[B + i * W : B + (i + 1) * W, :] if i < early else last
            right_ref[to, :] = base_right[to, :] + 0.1 * part
    to = pl.ds(pl.multiple_of(at_ref[2 + 2 * early + 1], W), W)
    right_ref[to, :] = base_right[to, :]


def sum_up(at, base_left, base_right, keep, got, own, last):
    out = jax.ShapeDtypeStruct(base_left.shape, f32)
    return pl.pallas_call(
        sum_kernel,
        out_shape=(out, out),
        in_specs=[SMEM] + [VMEM] * 6,
        out_specs=(VMEM, VMEM),
        scratch_shapes=[pltpu.VMEM((W, W), bf16)],
        compiler_params=PARAMS,
        cost_estimate=pl.CostEstimate(flops=WEIGHT, bytes_accessed=2**22, transcendentals=0),
    )(at, base_left, base_right, keep, got, own, last)


def finish_kernel(at_ref, left_ref, right_ref, own_ref, last_ref, out_ref, result, rows, sems):
    result[1] = right_ref[...]
    to = pl.ds(pl.multiple_of(at_ref[2 + 2 * (FIRST + SECOND) + 1], W), W)
    result[1, to, :] = right_ref[to, :] + 0.1 * right_of(last_ref[...], own_ref[...])
    copies = [pltpu.make_async_copy(result.at[1], out_ref.at[1], sems.at[0])]
    copies[0].start()
    rows[...] = last_ref[pl.ds(pl.multiple_of(at_ref[0], W), W), :]
    for i, start in enumerate(range(0, B, STRIP)):
        to = slice(start, start + STRIP)
        result[0, to, :] = left_ref[to, :] + 0.1 * left_of(last_ref, rows, start)
        copies.append(
            pltpu.make_async_copy(
                result.at[0, pl.ds(start, STRIP)], out_ref.at[0, pl.ds(start, STRIP)], sems.at[1 + i]
            )
        )
        copies[-1].start()
    for copy in copies:
        copy.wait()


def finish(at, left, right, own, last):
    return pl.pallas_call(
        finish_kernel,
        out_shape=jax.ShapeDtypeStruct((2, *left.shape), f32),
        in_specs=[SMEM] + [VMEM] * 4,
        out_specs=pl.BlockSpec(memory_space=pl.ANY),
        scratch_shapes=[
            pltpu.VMEM((2, *left.shape), f32),
            pltpu.VMEM((W, W), bf16),
            pltpu.SemaphoreType.DMA((1 + B // STRIP,)),
        ],
        compiler_params=PARAMS,
    )(at, left, right, own, last)


def ring(value, direction):
    pairs = [
        (x * 2 + core, (x + direction * (1 - 2 * core)) % 4 * 2 + core)
        for x in range(4)
        for core in range(2)
    ]
    return lax.ppermute(value, ("x", "core"), pairs)


def swap(value, axis):
    return lax.ppermute(value, axis, [(0, 1), (1, 0)])


def shards(grad, owner, codes, scale_ids, scale_table):
    rows_here, width_here = grad.shape
    slots = lax.axis_size("tensor")
    y, x, core = (lax.axis_index(name) for name in ("y", "x", "core"))
    chunks = grad.reshape(slots, rows_here // slots, width_here)
    spread = exchange(chunks)
    owner_row = lax.dynamic_index_in_dim(owner, lax.axis_index("c"), 0, keepdims=False)
    placed = place(spread, destinations(owner_row, core))
    own = exchange(placed).reshape(rows_here, width_here)
    base_left, base_right = (dequant(side, scale_table, codes, scale_ids) for side in range(2))

    def row_starts(core):
        step = 1 - 2 * core
        xs = [x, x - step, x + step, x, x - step, x + step, x + 2, x + 2]
        ys = [y, y, y, 1 - y, 1 - y, 1 - y, y, 1 - y]
        return [((row * 4 + column % 4) * 2 + core) * W for row, column in zip(ys, xs)]

    mine, theirs = row_starts(core), row_starts(1 - core)
    at = jnp.stack([mine[0], theirs[0]] + mine + theirs).astype(jnp.int32)
    across = swap(own, "y")
    behind = ring(own, 1)
    ahead = ring(own, -1)
    other = swap(own, "core")
    across, base_left = lax.optimization_barrier((across, base_left))
    across_ahead = ring(across, -1)
    behind, base_left = lax.optimization_barrier((behind, base_left))
    across_behind = swap(behind, "y")
    ahead, other, behind = lax.optimization_barrier((ahead, other, behind))
    far = ring(ahead, -1)
    left = first_grams(at, [own, behind, ahead, across])
    left, across_ahead = lax.optimization_barrier((left, across_ahead))
    across_far = ring(across_ahead, -1)
    right = middle_grams(own, other, [own, behind, ahead, across, across_behind])
    keep, send = second_grams(at, own, other, left, right, [across_behind, across_ahead, far])
    got, got_far = swap(send, "core"), swap(across_far, "core")
    left, right = sum_up(at, base_left, base_right, keep, got, own, across_far)
    return finish(at, left, right, own, got_far)


def solution(mesh):
    fine = Mesh(mesh.devices.reshape(4, 2, 4, 2, 8), ("c", "y", "x", "core", "tensor"))
    fsdp = ("c", "y", "x", "core")
    in_specs = (P("tensor", fsdp), P(), P(None, "tensor", fsdp), P(None, "tensor", fsdp), P())
    out_specs = P(None, "tensor", fsdp)
    return jax.shard_map(shards, mesh=fine, in_specs=in_specs, out_specs=out_specs, check_vma=False)
```

```python
import functools

import jax
import jax.numpy as jnp
from jax import lax
from jax.experimental import pallas as pl
from jax.experimental.pallas import tpu as pltpu
from jax.sharding import Mesh
from jax.sharding import PartitionSpec as P

B = 2048
W = 128
FIRST, MIDDLE, SECOND = 4, 5, 3
STRIP = 512
ORDERS = ((0, 4, 2, 6, 1, 5, 3, 7), (0, 4, 6, 2, 5, 1, 7, 3))
WEIGHT = 2**36
VMEM = pl.BlockSpec(memory_space=pltpu.VMEM)
SMEM = pl.BlockSpec(memory_space=pltpu.SMEM)
PARAMS = pltpu.CompilerParams(vmem_limit_bytes=20 * 2**20)
f32 = jnp.float32
bf16 = jnp.bfloat16


def place_kernel(places_ref, in_ref, out_ref):
    for i in range(in_ref.shape[0]):
        out_ref[pl.ds(places_ref[i], 1)] = in_ref[i : i + 1]


def place(chunks, places):
    return pl.pallas_call(
        place_kernel,
        out_shape=jax.ShapeDtypeStruct(chunks.shape, chunks.dtype),
        in_specs=[SMEM, VMEM],
        out_specs=VMEM,
        compiler_params=PARAMS,
    )(places, chunks)


def exchange(chunks):
    groups = [[core * len(order) + z for z in order] for core, order in enumerate(ORDERS)]
    return lax.all_to_all(chunks, ("core", "tensor"), 0, 0, axis_index_groups=groups, tiled=True)


def destinations(owner_row, core):
    order = jnp.where(core == 0, jnp.asarray(ORDERS[0], jnp.int32), jnp.asarray(ORDERS[1], jnp.int32))
    places = jnp.arange(order.shape[0], dtype=jnp.int32)
    slots = jnp.sum(jnp.where(order[:, None] == places, owner_row, 0), axis=1)
    return jnp.sum(jnp.where(slots[:, None] == order, places, 0), axis=1)


def scale_kernel(table_ref, ids_ref, out_ref):
    ids = ids_ref[...]
    scale = jnp.zeros(ids.shape, f32)
    for level in range(table_ref.shape[0]):
        scale = jnp.where(ids == level, table_ref[level], scale)
    out_ref[...] = scale


def scales(scale_table, scale_ids):
    return pl.pallas_call(
        scale_kernel,
        out_shape=jax.ShapeDtypeStruct(scale_ids.shape, f32),
        in_specs=[SMEM, VMEM],
        out_specs=VMEM,
        compiler_params=PARAMS,
        cost_estimate=pl.CostEstimate(flops=WEIGHT, bytes_accessed=2**15, transcendentals=0),
    )(scale_table, scale_ids)


def dequant_kernel(codes_ref, scale_ref, left_ref, right_ref):
    groups = scale_ref.shape[1]
    group_rows = codes_ref.shape[1] // groups
    for side, out_ref in enumerate((left_ref, right_ref)):
        for group in range(groups):
            rows = slice(group * group_rows, (group + 1) * group_rows)
            code = codes_ref[side, rows, :].astype(f32)
            scale = scale_ref[side, group : group + 1, :]
            out_ref[rows, :] = 0.9 * (scale * ((code - 7.5) / 7.5))


def dequant(codes, scale):
    out = jax.ShapeDtypeStruct(codes.shape[1:], f32)
    return pl.pallas_call(
        dequant_kernel,
        out_shape=(out, out),
        in_specs=[VMEM, VMEM],
        out_specs=(VMEM, VMEM),
        compiler_params=PARAMS,
        cost_estimate=pl.CostEstimate(flops=WEIGHT, bytes_accessed=2**22, transcendentals=0),
    )(codes, scale)


def left_of(block, rows, start):
    return lax.dot_general(
        block[start : start + STRIP, :],
        rows[...],
        (((1,), (1,)), ((), ())),
        preferred_element_type=f32,
    )


def right_of(piece, pair):
    return lax.dot_general(piece, pair, (((0,), (0,)), ((), ())), preferred_element_type=f32)


def collect(at_ref, pieces, block, rows):
    for i, piece in enumerate(pieces):
        block[:, i * W : (i + 1) * W] = piece[...]
    for i in range(2):
        rows[i * W : (i + 1) * W, :] = block[pl.ds(pl.multiple_of(at_ref[i], W), W), :]


def first_kernel(at_ref, *refs):
    pieces, (left_ref, block, rows) = refs[:FIRST], refs[FIRST:]
    collect(at_ref, pieces, block, rows)
    for start in range(0, B, STRIP):
        left_ref[start : start + STRIP, :] = left_of(block, rows, start)


def first_grams(at, pieces):
    return pl.pallas_call(
        first_kernel,
        out_shape=jax.ShapeDtypeStruct((B, 2 * W), f32),
        in_specs=[SMEM] + [VMEM] * FIRST,
        out_specs=VMEM,
        scratch_shapes=[pltpu.VMEM((B, FIRST * W), bf16), pltpu.VMEM((2 * W, FIRST * W), bf16)],
        compiler_params=PARAMS,
        cost_estimate=pl.CostEstimate(flops=2**30, bytes_accessed=2**22, transcendentals=0),
    )(at, *pieces)


def middle_kernel(own_ref, other_ref, *refs):
    pieces, (right_ref, pair) = refs[:MIDDLE], refs[MIDDLE:]
    pair[:, :W] = own_ref[...]
    pair[:, W:] = other_ref[...]
    for i, piece in enumerate(pieces):
        right_ref[i * W : (i + 1) * W, :] = right_of(piece[...], pair[...])


def middle_grams(own, other, pieces):
    return pl.pallas_call(
        middle_kernel,
        out_shape=jax.ShapeDtypeStruct((MIDDLE * W, 2 * W), f32),
        in_specs=[VMEM] * (2 + MIDDLE),
        out_specs=VMEM,
        scratch_shapes=[pltpu.VMEM((B, 2 * W), bf16)],
        compiler_params=PARAMS,
        cost_estimate=pl.CostEstimate(flops=2**30, bytes_accessed=2**22, transcendentals=0),
    )(own, other, *pieces)


def second_kernel(at_ref, own_ref, other_ref, left_ref, right_ref, *refs):
    pieces, (keep_ref, send_ref, block, pair, rows) = refs[:SECOND], refs[SECOND:]
    collect(at_ref, pieces, block, rows)
    pair[:, :W] = own_ref[...]
    pair[:, W:] = other_ref[...]
    for start in range(0, B, STRIP):
        to = slice(start, start + STRIP)
        left = left_ref[to, :] + left_of(block, rows, start)
        keep_ref[to, :] = left[:, :W]
        send_ref[to, :] = left[:, W:]
    middle = B + MIDDLE * W
    keep_ref[B:middle, :] = right_ref[:, :W]
    send_ref[B:middle, :] = right_ref[:, W:]
    for i, piece in enumerate(pieces[MIDDLE - FIRST :]):
        to = slice(middle + i * W, middle + (i + 1) * W)
        right = right_of(piece[...], pair[...])
        keep_ref[to, :] = right[:, :W]
        send_ref[to, :] = right[:, W:]


def second_grams(at, own, other, left, right, pieces):
    out = jax.ShapeDtypeStruct((B + (FIRST + SECOND) * W, W), f32)
    return pl.pallas_call(
        second_kernel,
        out_shape=(out, out),
        in_specs=[SMEM] + [VMEM] * (4 + SECOND),
        out_specs=(VMEM, VMEM),
        scratch_shapes=[
            pltpu.VMEM((B, SECOND * W), bf16),
            pltpu.VMEM((B, 2 * W), bf16),
            pltpu.VMEM((2 * W, SECOND * W), bf16),
        ],
        compiler_params=PARAMS,
        cost_estimate=pl.CostEstimate(flops=2**30, bytes_accessed=2**22, transcendentals=0),
    )(at, own, other, left, right, *pieces)


def sum_kernel(at_ref, base_left, base_right, keep_ref, got_ref, own_ref, last_ref, left_ref, right_ref, rows):
    rows[...] = last_ref[pl.ds(pl.multiple_of(at_ref[0], W), W), :]
    for start in range(0, B, STRIP):
        to = slice(start, start + STRIP)
        left = keep_ref[to, :] + got_ref[to, :] + left_of(last_ref, rows, start)
        left_ref[to, :] = base_left[to, :] + 0.1 * left
    last = right_of(last_ref[...], own_ref[...])
    early = FIRST + SECOND
    for side, part_ref in enumerate((keep_ref, got_ref)):
        for i in range(early + 1 - side):
            to = pl.ds(pl.multiple_of(at_ref[2 + side * (early + 1) + i], W), W)
            part = part_ref[B + i * W : B + (i + 1) * W, :] if i < early else last
            right_ref[to, :] = base_right[to, :] + 0.1 * part
    to = pl.ds(pl.multiple_of(at_ref[2 + 2 * early + 1], W), W)
    right_ref[to, :] = base_right[to, :]


def sum_up(at, base_left, base_right, keep, got, own, last):
    out = jax.ShapeDtypeStruct(base_left.shape, f32)
    return pl.pallas_call(
        sum_kernel,
        out_shape=(out, out),
        in_specs=[SMEM] + [VMEM] * 6,
        out_specs=(VMEM, VMEM),
        scratch_shapes=[pltpu.VMEM((W, W), bf16)],
        compiler_params=PARAMS,
        cost_estimate=pl.CostEstimate(flops=WEIGHT, bytes_accessed=2**22, transcendentals=0),
    )(at, base_left, base_right, keep, got, own, last)


def finish_kernel(at_ref, left_ref, right_ref, own_ref, last_ref, out_ref, result, rows, sems):
    result[1] = right_ref[...]
    to = pl.ds(pl.multiple_of(at_ref[2 + 2 * (FIRST + SECOND) + 1], W), W)
    result[1, to, :] = right_ref[to, :] + 0.1 * right_of(last_ref[...], own_ref[...])
    copies = [pltpu.make_async_copy(result.at[1], out_ref.at[1], sems.at[0])]
    copies[0].start()
    rows[...] = last_ref[pl.ds(pl.multiple_of(at_ref[0], W), W), :]
    for i, start in enumerate(range(0, B, STRIP)):
        to = slice(start, start + STRIP)
        result[0, to, :] = left_ref[to, :] + 0.1 * left_of(last_ref, rows, start)
        copies.append(
            pltpu.make_async_copy(
                result.at[0, pl.ds(start, STRIP)], out_ref.at[0, pl.ds(start, STRIP)], sems.at[1 + i]
            )
        )
        copies[-1].start()
    for copy in copies:
        copy.wait()


def finish(at, left, right, own, last):
    return pl.pallas_call(
        finish_kernel,
        out_shape=jax.ShapeDtypeStruct((2, *left.shape), f32),
        in_specs=[SMEM] + [VMEM] * 4,
        out_specs=pl.BlockSpec(memory_space=pl.ANY),
        scratch_shapes=[
            pltpu.VMEM((2, *left.shape), f32),
            pltpu.VMEM((W, W), bf16),
            pltpu.SemaphoreType.DMA((1 + B // STRIP,)),
        ],
        compiler_params=PARAMS,
    )(at, left, right, own, last)


def ring(value, direction):
    pairs = [
        (x * 2 + core, (x + direction * (1 - 2 * core)) % 4 * 2 + core)
        for x in range(4)
        for core in range(2)
    ]
    return lax.ppermute(value, ("x", "core"), pairs)


def swap(value, axis):
    return lax.ppermute(value, axis, [(0, 1), (1, 0)])


def shards(grad, owner, codes, scale_ids, scale_table):
    rows_here, width_here = grad.shape
    slots = lax.axis_size("tensor")
    y, x, core = (lax.axis_index(name) for name in ("y", "x", "core"))
    chunks = grad.reshape(slots, rows_here // slots, width_here)
    spread = exchange(chunks)
    owner_row = lax.dynamic_index_in_dim(owner, lax.axis_index("c"), 0, keepdims=False)
    placed = place(spread, destinations(owner_row, core))
    own = exchange(placed).reshape(rows_here, width_here)
    scale = scales(scale_table, scale_ids)

    def row_starts(core):
        step = 1 - 2 * core
        xs = [x, x - step, x + step, x, x - step, x + step, x + 2, x + 2]
        ys = [y, y, y, 1 - y, 1 - y, 1 - y, y, 1 - y]
        return [((row * 4 + column % 4) * 2 + core) * W for row, column in zip(ys, xs)]

    mine, theirs = row_starts(core), row_starts(1 - core)
    at = jnp.stack([mine[0], theirs[0]] + mine + theirs).astype(jnp.int32)
    across = swap(own, "y")
    behind = ring(own, 1)
    ahead = ring(own, -1)
    other = swap(own, "core")
    across, scale = lax.optimization_barrier((across, scale))
    across_ahead = ring(across, -1)
    behind, scale = lax.optimization_barrier((behind, scale))
    across_behind = swap(behind, "y")
    ahead, other, behind = lax.optimization_barrier((ahead, other, behind))
    far = ring(ahead, -1)
    left = first_grams(at, [own, behind, ahead, across])
    left, across_ahead = lax.optimization_barrier((left, across_ahead))
    across_far = ring(across_ahead, -1)
    right = middle_grams(own, other, [own, behind, ahead, across, across_behind])
    keep, send = second_grams(at, own, other, left, right, [across_behind, across_ahead, far])
    got, got_far = swap(send, "core"), swap(across_far, "core")
    base_left, base_right = dequant(codes, scale)
    left, right = sum_up(at, base_left, base_right, keep, got, own, across_far)
    return finish(at, left, right, own, got_far)


def solution(mesh):
    fine = Mesh(mesh.devices.reshape(4, 2, 4, 2, 8), ("c", "y", "x", "core", "tensor"))
    fsdp = ("c", "y", "x", "core")
    in_specs = (P("tensor", fsdp), P(), P(None, "tensor", fsdp), P(None, "tensor", fsdp), P())
    out_specs = P(None, "tensor", fsdp)
    return jax.shard_map(shards, mesh=fine, in_specs=in_specs, out_specs=out_specs, check_vma=False)
```
